32 devices in a mesh: row: 2 (over core), col: 16 (over z, y, x).
Axes of the slice: x: 2, y: 2, z: 4, core: 2. Of those that a mesh axis runs over, the one named last changes fastest.
Arguments:
- pair_activations: bfloat16 [1024, 1024, 128], P('row', 'col'), may hold values from -40 to 40
- pair_logit_weight: bfloat16 [128, 8], replicated, may hold values from -0.7 to 0.7
- normed_strand_features: bfloat16 [256, 1024, 64], P('row', 'col'), may hold values from -6 to 6
- mean_output_sensitivity: bfloat16 [256, 1024, 64], P('col', 'row'), may hold values from -96 to 96
- projected_entries: bfloat16 [64, 64], replicated, may hold values from -0.75 to 0.75
Outputs:
- d_pair: bfloat16 [1024, 1024, 128], P('row', 'col')
- grad_pair_weight: float32 [128, 8], replicated
- value_weight_gradient: float32 [64, 64], replicated
The draws below stay inside these ranges and needn't reach their ends.
All inputs are finite; a program needn't handle non-finite values.
Results may differ from the reference program's by a relative error of at most 0.018.
Values may be sent and summed in bfloat16 or wider, within the bound.
A program may use at most 128 MiB of HBM per device.

```python
import jax
import jax.numpy as jnp
from jax import lax

CZ = 128
FEATURE_BREADTH = 64
H = 8
C = 8
RESIDUE_TALLY = 1024
ALIGNED_STRANDS = 256
N_ROW = 2


def common_signs(key):
    return 2.0 * jax.random.randint(key, (CZ,), 0, 2).astype(jnp.float32) - 1.0


def draw_pair_logit_weight(key, part):
    signs = common_signs(key)
    key = jax.random.fold_in(key, 5)
    noise = jnp.clip(jax.random.normal(key, (CZ, H)), -3.0, 3.0)
    return ((noise + 0.5 * signs[:, None]) / CZ ** 0.5).astype(jnp.bfloat16)


def draw_pair_activations(key, part):
    key = jax.random.fold_in(key, 11)
    noise_key, row_key, col_key = jax.random.split(key, 3)
    position = jnp.arange(RESIDUE_TALLY, dtype=jnp.float32) / max(RESIDUE_TALLY - 1, 1)
    row_scale = 3.0 ** (0.5 * position) * jax.random.uniform(row_key, (RESIDUE_TALLY,), minval=0.8, maxval=1.25)
    col_scale = 3.0 ** (0.5 * position) * jax.random.uniform(col_key, (RESIDUE_TALLY,), minval=0.8, maxval=1.25)
    noise = jnp.clip(jax.random.normal(noise_key, (RESIDUE_TALLY, RESIDUE_TALLY, CZ)), -6.0, 6.0)
    return (noise * row_scale[:, None, None] * col_scale[None, :, None]).astype(jnp.bfloat16)


def level_of(rng, dims, shards, smallest, top_value):
    def one(axis_at, shards_of):
        heights = jax.random.uniform(jax.random.fold_in(jax.random.fold_in(rng, 6), axis_at), (shards_of,), jnp.float32, smallest / len(shards), top_value / len(shards))
        return jnp.repeat(jnp.exp(heights), dims[axis_at] // shards_of).reshape((-1,) + (1,) * (len(dims) - axis_at - 1))

    gain = one(*shards[0])
    for cut in shards[1:]:
        gain = gain * one(*cut)
    return gain


def normal_values(rng, shape, spread, limit, cuts=(), held_as=jnp.bfloat16):
    values = spread * jax.random.normal(rng, shape, jnp.float32)
    if cuts:
        values = values * level_of(rng, shape, cuts, -0.22, 0.18)
    return jnp.clip(values, -limit, limit).astype(held_as)


def setup_inputs(seed: int = 0) -> dict:
    splits = jax.random.split(jax.random.key(seed), 6)
    pair_activations = draw_pair_activations(jax.random.fold_in(splits[5], 71), 0)
    pair_logit_weight = draw_pair_logit_weight(jax.random.fold_in(splits[5], 71), 0)
    normed_strand_features = normal_values(splits[2], (ALIGNED_STRANDS, RESIDUE_TALLY, FEATURE_BREADTH), 1.0, 6.0, ((0, 2), (1, 16)))
    mean_output_sensitivity = normal_values(splits[3], (ALIGNED_STRANDS, RESIDUE_TALLY, FEATURE_BREADTH), (RESIDUE_TALLY / 64), 96.0, ((0, 16), (1, 2)))
    projected_entries = normal_values(splits[4], (FEATURE_BREADTH, FEATURE_BREADTH), FEATURE_BREADTH ** -0.5, 0.75)
    return {"pair_activations": pair_activations, "pair_logit_weight": pair_logit_weight, "normed_strand_features": normed_strand_features, "mean_output_sensitivity": mean_output_sensitivity, "projected_entries": projected_entries}


HIGH_PRECISION = lax.Precision.HIGHEST


def reference(pair_activations, pair_logit_weight, normed_strand_features, mean_output_sensitivity, projected_entries):
    projected_strand_lines = jnp.dot(normed_strand_features.reshape(ALIGNED_STRANDS * RESIDUE_TALLY, FEATURE_BREADTH), projected_entries, preferred_element_type=jnp.float32).astype(jnp.bfloat16)
    projected_strand_lines = projected_strand_lines.astype(jnp.float32).reshape(ALIGNED_STRANDS, RESIDUE_TALLY, H, C)
    grads = mean_output_sensitivity.astype(jnp.float32).reshape(ALIGNED_STRANDS, RESIDUE_TALLY, H, C)
    weight_wide = pair_logit_weight.astype(jnp.float32)
    block = RESIDUE_TALLY // N_ROW

    def block_step(running, block_index):
        d_values_acc, d_pair_weight_acc = running
        first = (block_index * block).astype(jnp.int32)
        pair_block = lax.dynamic_slice_in_dim(pair_activations, first, block, 0).astype(jnp.float32)
        logits = jnp.einsum("ijk,kh->ijh", pair_block, weight_wide, precision=HIGH_PRECISION)
        row_max = jnp.max(logits, axis=1)
        exponent = jnp.exp(logits - row_max[:, None, :])
        row_total = jnp.sum(exponent, axis=1)
        probs = exponent / row_total[:, None, :]
        grad_block = lax.dynamic_slice_in_dim(grads, first, block, 1)
        d_probs = jnp.einsum("sihc,sjhc->ijh", grad_block, projected_strand_lines, precision=HIGH_PRECISION)
        row_dot = jnp.sum(probs * d_probs, axis=1)
        d_logits = probs * (d_probs - row_dot[:, None, :])
        d_logits_low = d_logits.astype(jnp.bfloat16).astype(jnp.float32)
        d_pair_block = jnp.einsum("ijh,kh->ijk", d_logits_low, weight_wide, precision=HIGH_PRECISION).astype(jnp.bfloat16)
        d_pair_weight = jnp.einsum("ijk,ijh->kh", pair_block, d_logits_low, precision=HIGH_PRECISION)
        probs_low = lax.optimization_barrier(probs.astype(jnp.bfloat16)).astype(jnp.float32)
        projected_entry_sensitivity = jnp.einsum("ijh,sihc->sjhc", probs_low, grad_block, precision=HIGH_PRECISION)
        return (d_values_acc + projected_entry_sensitivity, d_pair_weight_acc + d_pair_weight), d_pair_block

    initial = (jnp.zeros((ALIGNED_STRANDS, RESIDUE_TALLY, H, C), jnp.float32), jnp.zeros((CZ, H), jnp.float32))
    (projected_entry_sensitivity, d_pair_weight), d_pair_blocks = lax.scan(block_step, initial, jnp.arange(N_ROW, dtype=jnp.int32))
    d_pair = d_pair_blocks.reshape(RESIDUE_TALLY, RESIDUE_TALLY, CZ)
    projected_entry_sensitivity_folded = projected_entry_sensitivity.astype(jnp.bfloat16).astype(jnp.float32).reshape(ALIGNED_STRANDS, RESIDUE_TALLY, FEATURE_BREADTH)
    value_weight_gradient = jnp.einsum("dxr,dxt->rt", normed_strand_features.astype(jnp.float32), projected_entry_sensitivity_folded, precision=HIGH_PRECISION)
    return d_pair, d_pair_weight / RESIDUE_TALLY, value_weight_gradient / RESIDUE_TALLY
```

```python
import functools
import math

import jax
import jax.numpy as jnp
from jax import lax
from jax.experimental import pallas as pl
from jax.experimental.pallas import tpu as pltpu
from jax.sharding import PartitionSpec as P

MESH = pl.DeviceIdType.MESH
VMEM_BYTES = 48 * 1024 * 1024


def exchange_kernel(axes, combine, mine, out, slots, send, recv):
    sizes = [lax.axis_size(a) for a in axes]
    n = math.prod(sizes)
    me = lax.axis_index(axes[0])
    for a, size in zip(axes[1:], sizes[1:]):
        me = me * size + lax.axis_index(a)

    def device(p):
        if len(axes) == 1:
            return {axes[0]: p}
        return {axes[0]: p // sizes[1], axes[1]: p % sizes[1]}

    barrier = pltpu.get_barrier_semaphore()

    def greet(d, carry):
        pl.semaphore_signal(barrier, inc=1, device_id=device(lax.rem(me + d, n)), device_id_type=MESH)
        return carry

    lax.fori_loop(1, n, greet, 0)
    pl.semaphore_wait(barrier, n - 1)

    def copy(to, slot):
        return pltpu.make_async_remote_copy(
            src_ref=mine, dst_ref=slots.at[slot], send_sem=send.at[to], recv_sem=recv.at[slot],
            device_id=device(to), device_id_type=MESH)

    def begin(d, carry):
        copy(lax.rem(me + d, n), me).start()
        return carry

    lax.fori_loop(1, n, begin, 0)
    slots[me] = mine[...]

    def finish(d, carry):
        peer = lax.rem(me + d, n)
        copy(peer, peer).wait_recv()
        copy(peer, me).wait_send()
        return carry

    lax.fori_loop(1, n, finish, 0)
    combine(n, slots, out)


def add_up(n, slots, out):
    out[...] = lax.fori_loop(1, n, lambda p, total: total + slots[p], slots[0])


def join_softmax(n, slots, out):
    top = lax.fori_loop(1, n, lambda p, m: jnp.maximum(m, slots[p, 0]), slots[0, 0])
    total = lax.fori_loop(
        0, n, lambda p, t: t + slots[p, 1] * jnp.exp(slots[p, 0] - top), jnp.zeros_like(top))
    out[0] = top
    out[1] = total


def exchange(x, axes, combine, collective_id):
    n = math.prod(lax.axis_size(a) for a in axes)
    return pl.pallas_call(
        functools.partial(exchange_kernel, axes, combine),
        out_shape=jax.ShapeDtypeStruct(x.shape, x.dtype),
        in_specs=[pl.BlockSpec(memory_space=pltpu.VMEM)],
        out_specs=pl.BlockSpec(memory_space=pltpu.VMEM),
        scratch_shapes=[
            pltpu.VMEM((n,) + x.shape, x.dtype),
            pltpu.SemaphoreType.DMA((n,)),
            pltpu.SemaphoreType.DMA((n,)),
        ],
        compiler_params=pltpu.CompilerParams(
            collective_id=collective_id, has_side_effects=True, vmem_limit_bytes=VMEM_BYTES),
    )(x)


def strand_kernel(heads, strands, g, v, p, f, d_probs, dot, weight, p_low, d_values):
    step = pl.program_id(0)
    tokens, lanes = p.shape[1], g.shape[3]

    @pl.when(step == 0)
    def _():
        p_low[...] = p[...].astype(jnp.bfloat16)
        d_probs[...] = jnp.zeros_like(d_probs)

    rows = pl.ds(pl.multiple_of(step * tokens, tokens), tokens)
    for h in range(heads):
        d_probs[h] += lax.dot_general(
            v[h], g[0, h], (((1,), (1,)), ((), ())), preferred_element_type=jnp.float32)
        d_values[rows, h * lanes:(h + 1) * lanes] = jnp.dot(
            p_low[h], g[0, h], preferred_element_type=jnp.float32).astype(jnp.bfloat16)

    @pl.when(step == pl.num_programs(0) - 1)
    def _():
        dot[...] = jnp.sum(p[...] * d_probs[...], axis=1)
        width = f.shape[0] // strands
        head_width = lanes // strands
        strand_of_lane = (lax.broadcasted_iota(jnp.int32, (width, heads * lanes), 1) % lanes) // head_width
        part = strands // 4
        total = jnp.zeros((width, heads * lanes), jnp.float32)
        for q in range(4):
            cross = jnp.dot(
                f[q * part * width:(q + 1) * part * width, :], d_values[...],
                preferred_element_type=jnp.float32)
            for s in range(part):
                total += jnp.where(
                    strand_of_lane == q * part + s, cross[s * width:(s + 1) * width], 0.0)
        weight[...] = total


def strand_sums(g, v, p, f, strands):
    steps, heads, rows, lanes = g.shape
    tokens = p.shape[1]
    width = f.shape[0] // strands
    whole = lambda shape: pl.BlockSpec(shape, lambda c: (0,) * len(shape))
    return pl.pallas_call(
        functools.partial(strand_kernel, heads, strands),
        grid=(steps,),
        in_specs=[
            pl.BlockSpec((1, heads, rows, lanes), lambda c: (c, 0, 0, 0)),
            pl.BlockSpec((heads, tokens, lanes), lambda c: (0, 0, c)),
            whole(p.shape),
            whole(f.shape),
        ],
        out_specs=[whole(p.shape), whole((heads, rows)), whole((width, heads * lanes))],
        out_shape=[
            jax.ShapeDtypeStruct(p.shape, jnp.float32),
            jax.ShapeDtypeStruct((heads, rows), jnp.float32),
            jax.ShapeDtypeStruct((width, heads * lanes), jnp.float32),
        ],
        scratch_shapes=[
            pltpu.VMEM(p.shape, jnp.bfloat16),
            pltpu.VMEM((steps * tokens, heads * lanes), jnp.bfloat16),
        ],
        compiler_params=pltpu.CompilerParams(vmem_limit_bytes=VMEM_BYTES),
    )(g, v, p, f)


def on_device(pair, pair_weight, features, sensitivity, entries):
    rows, tokens, pair_width = pair.shape
    heads = pair_weight.shape[1]
    strands, _, width = sensitivity.shape
    head_width = width // heads
    blocks = lax.axis_size("col")
    token_total = tokens * blocks
    lanes = strands * head_width

    g = sensitivity.reshape(strands, rows, heads, head_width)
    g = g.transpose(2, 1, 0, 3).reshape(heads, rows, lanes)
    g = lax.all_gather(g, "col", axis=0)

    everyone = lax.all_gather(features, "row", axis=0, tiled=True)
    logits = jnp.einsum("ijk,kh->hji", pair, pair_weight, preferred_element_type=jnp.float32)
    local_max = jnp.max(logits, axis=1)
    local_total = jnp.sum(jnp.exp(logits - local_max[:, None, :]), axis=1)
    joined = exchange(jnp.stack([local_max, local_total]), ("col",), join_softmax, 1)
    probs = jnp.exp(logits - joined[0][:, None, :]) / joined[1][:, None, :]

    v = jnp.dot(everyone.reshape(-1, width), entries, preferred_element_type=jnp.float32)
    v = v.astype(jnp.bfloat16).reshape(blocks, strands, tokens, heads, head_width)
    v = v.transpose(3, 2, 0, 1, 4).reshape(heads, tokens, blocks * lanes)
    f = everyone.reshape(blocks, strands, tokens, width)
    f = f.transpose(1, 3, 0, 2).reshape(strands * width, blocks * tokens)

    d_probs, dot, crossed = strand_sums(g, v, probs, f, strands)
    row_dot = exchange(dot, ("col",), add_up, 2)
    d_logits = (probs * (d_probs - row_dot[:, None, :])).astype(jnp.bfloat16)
    d_pair = jnp.einsum(
        "hji,kh->ijk", d_logits, pair_weight, preferred_element_type=jnp.float32
    ).astype(jnp.bfloat16)
    d_pair_weight = jnp.einsum("ijk,hji->hk", pair, d_logits, preferred_element_type=jnp.float32)
    d_value_weight = crossed.reshape(width, heads, strands, head_width).sum(2)
    both = jnp.concatenate([d_pair_weight.reshape(-1), d_value_weight.reshape(-1)])
    both = exchange(both.reshape(-1, 128), ("row", "col"), add_up, 3).reshape(-1)
    both = both * (1.0 / token_total)
    cut = heads * pair_width
    return (
        d_pair,
        both[:cut].reshape(heads, pair_width).T,
        both[cut:].reshape(width, width),
    )


def solution(mesh):
    placed = (P("row", "col", None), P(), P("row", "col", None), P("col", "row", None), P())
    return jax.shard_map(
        on_device,
        mesh=mesh,
        in_specs=placed,
        out_specs=(P("row", "col", None), P(), P()),
        check_vma=False,
    )
```

```python
import functools
import math

import jax
import jax.numpy as jnp
from jax import lax
from jax.experimental import pallas as pl
from jax.experimental.pallas import tpu as pltpu
from jax.sharding import PartitionSpec as P

MESH = pl.DeviceIdType.MESH
VMEM_BYTES = 48 * 1024 * 1024


def exchange_kernel(axes, combine, mine, out, slots, send, recv):
    sizes = [lax.axis_size(a) for a in axes]
    n = math.prod(sizes)
    me = lax.axis_index(axes[0])
    for a, size in zip(axes[1:], sizes[1:]):
        me = me * size + lax.axis_index(a)

    def device(p):
        if len(axes) == 1:
            return {axes[0]: p}
        return {axes[0]: p // sizes[1], axes[1]: p % sizes[1]}

    barrier = pltpu.get_barrier_semaphore()

    def greet(d, carry):
        pl.semaphore_signal(barrier, inc=1, device_id=device(lax.rem(me + d, n)), device_id_type=MESH)
        return carry

    lax.fori_loop(1, n, greet, 0)
    pl.semaphore_wait(barrier, n - 1)

    def copy(to, slot):
        return pltpu.make_async_remote_copy(
            src_ref=mine, dst_ref=slots.at[slot], send_sem=send.at[to], recv_sem=recv.at[slot],
            device_id=device(to), device_id_type=MESH)

    def begin(d, carry):
        copy(lax.rem(me + d, n), me).start()
        return carry

    lax.fori_loop(1, n, begin, 0)
    slots[me] = mine[...]

    def finish(d, carry):
        peer = lax.rem(me + d, n)
        copy(peer, peer).wait_recv()
        copy(peer, me).wait_send()
        return carry

    lax.fori_loop(1, n, finish, 0)
    combine(n, slots, out)


def add_up(n, slots, out):
    out[...] = lax.fori_loop(1, n, lambda p, total: total + slots[p], slots[0])


def join_softmax(n, slots, out):
    top = lax.fori_loop(1, n, lambda p, m: jnp.maximum(m, slots[p, 0]), slots[0, 0])
    total = lax.fori_loop(
        0, n, lambda p, t: t + slots[p, 1] * jnp.exp(slots[p, 0] - top), jnp.zeros_like(top))
    out[0] = top
    out[1] = total


def exchange(x, axes, combine, collective_id):
    n = math.prod(lax.axis_size(a) for a in axes)
    return pl.pallas_call(
        functools.partial(exchange_kernel, axes, combine),
        out_shape=jax.ShapeDtypeStruct(x.shape, x.dtype),
        in_specs=[pl.BlockSpec(memory_space=pltpu.VMEM)],
        out_specs=pl.BlockSpec(memory_space=pltpu.VMEM),
        scratch_shapes=[
            pltpu.VMEM((n,) + x.shape, x.dtype),
            pltpu.SemaphoreType.DMA((n,)),
            pltpu.SemaphoreType.DMA((n,)),
        ],
        compiler_params=pltpu.CompilerParams(
            collective_id=collective_id, has_side_effects=True, vmem_limit_bytes=VMEM_BYTES),
    )(x)


def d_probs_kernel(heads, own, g, v, d_own, d_other, total):
    step = pl.program_id(0)

    @pl.when(step == 0)
    def _():
        total[...] = jnp.zeros_like(total)

    for h in range(heads):
        total[h] += lax.dot_general(
            v[h], g[0, h], (((1,), (1,)), ((), ())), preferred_element_type=jnp.float32)

    @pl.when(step == pl.num_programs(0) - 1)
    def _():
        d_own[...] = total[:, :own]
        d_other[...] = total[:, own:].astype(jnp.bfloat16)


def whole(shape):
    return pl.BlockSpec(shape, lambda c: (0,) * len(shape))


def d_probs_of(g, v):
    steps, heads, rows, lanes = g.shape
    tokens = v.shape[1]
    half = (heads, tokens // 2, rows)
    return pl.pallas_call(
        functools.partial(d_probs_kernel, heads, tokens // 2),
        grid=(steps,),
        in_specs=[
            pl.BlockSpec((1, heads, rows, lanes), lambda c: (c, 0, 0, 0)),
            pl.BlockSpec((heads, tokens, lanes), lambda c: (0, 0, c)),
        ],
        out_specs=[whole(half), whole(half)],
        out_shape=[jax.ShapeDtypeStruct(half, jnp.float32), jax.ShapeDtypeStruct(half, jnp.bfloat16)],
        scratch_shapes=[pltpu.VMEM((heads, tokens, rows), jnp.float32)],
        compiler_params=pltpu.CompilerParams(vmem_limit_bytes=VMEM_BYTES),
        cost_estimate=pl.CostEstimate(
            flops=2 * g.size * tokens, bytes_accessed=2 * g.size, transcendentals=0),
    )(g, v)


def value_kernel(heads, strands, g, p, f, weight, d_values):
    step = pl.program_id(0)
    tokens, lanes = p.shape[1], g.shape[3]
    rows = pl.ds(pl.multiple_of(step * tokens, tokens), tokens)
    for h in range(heads):
        d_values[rows, h * lanes:(h + 1) * lanes] = jnp.dot(
            p[h], g[0, h], preferred_element_type=jnp.float32).astype(jnp.bfloat16)

    @pl.when(step == pl.num_programs(0) - 1)
    def _():
        width = f.shape[0] // strands
        head_width = lanes // strands
        strand_of_lane = (lax.broadcasted_iota(jnp.int32, (width, heads * lanes), 1) % lanes) // head_width
        part = strands // 4
        total = jnp.zeros((width, heads * lanes), jnp.float32)
        for q in range(4):
            cross = jnp.dot(
                f[q * part * width:(q + 1) * part * width, :], d_values[...],
                preferred_element_type=jnp.float32)
            for s in range(part):
                total += jnp.where(
                    strand_of_lane == q * part + s, cross[s * width:(s + 1) * width], 0.0)
        weight[...] = total


def value_weight_of(g, p, f, strands):
    steps, heads, rows, lanes = g.shape
    tokens = p.shape[1]
    width = f.shape[0] // strands
    return pl.pallas_call(
        functools.partial(value_kernel, heads, strands),
        grid=(steps,),
        in_specs=[
            pl.BlockSpec((1, heads, rows, lanes), lambda c: (c, 0, 0, 0)),
            whole(p.shape),
            whole(f.shape),
        ],
        out_specs=whole((width, heads * lanes)),
        out_shape=jax.ShapeDtypeStruct((width, heads * lanes), jnp.float32),
        scratch_shapes=[pltpu.VMEM((steps * tokens, heads * lanes), jnp.bfloat16)],
        compiler_params=pltpu.CompilerParams(vmem_limit_bytes=VMEM_BYTES),
        cost_estimate=pl.CostEstimate(
            flops=4 * g.size * tokens, bytes_accessed=2 * g.size, transcendentals=0),
    )(g, p, f)


def pair_kernel(d_logits, pair, weight, d_pair, d_weight):
    @pl.when(pl.program_id(0) == 0)
    def _():
        d_weight[...] = jnp.zeros_like(d_weight)

    d_pair[...] = lax.dot_general(
        d_logits[...], weight[...], (((0,), (0,)), ((), ())), preferred_element_type=jnp.float32
    ).astype(jnp.bfloat16)
    d_weight[...] += jnp.dot(d_logits[...], pair[...], preferred_element_type=jnp.float32)


def pair_gradients(d_logits, pair, weight):
    heads, cells = d_logits.shape
    width = pair.shape[1]
    block = 4096
    return pl.pallas_call(
        pair_kernel,
        grid=(cells // block,),
        in_specs=[
            pl.BlockSpec((heads, block), lambda c: (0, c)),
            pl.BlockSpec((block, width), lambda c: (c, 0)),
            whole((heads, width)),
        ],
        out_specs=[pl.BlockSpec((block, width), lambda c: (c, 0)), whole((heads, width))],
        out_shape=[
            jax.ShapeDtypeStruct((cells, width), jnp.bfloat16),
            jax.ShapeDtypeStruct((heads, width), jnp.float32),
        ],
        compiler_params=pltpu.CompilerParams(vmem_limit_bytes=VMEM_BYTES),
    )(d_logits, pair, weight)


def on_device(pair, pair_weight, features, sensitivity, entries):
    rows, tokens, pair_width = pair.shape
    heads = pair_weight.shape[1]
    strands, _, width = sensitivity.shape
    head_width = width // heads
    blocks = lax.axis_size("col")
    token_total = tokens * blocks
    lanes = strands * head_width
    parity = lax.axis_index("col") % 2
    groups = [list(range(q, blocks, 2)) for q in range(2)]
    partners = [(c, c ^ 1) for c in range(blocks)]

    features = features.reshape(-1, 2, strands, tokens, width)
    kept = lax.dynamic_index_in_dim(features, parity, 1, keepdims=False)
    sent = lax.dynamic_index_in_dim(features, 1 - parity, 1, keepdims=False)
    both_tokens = jnp.concatenate([kept, lax.ppermute(sent, "col", partners)], axis=2)

    g = sensitivity.reshape(strands, rows, heads, head_width)
    g = g.transpose(2, 1, 0, 3).reshape(heads, rows, lanes)
    g = lax.all_gather(g, "col", axis=0, axis_index_groups=groups)

    everyone = lax.all_gather(both_tokens, "row", axis=0, tiled=True)
    logits = jnp.einsum("ijk,kh->hji", pair, pair_weight, preferred_element_type=jnp.float32)
    local_max = jnp.max(logits, axis=1)
    local_total = jnp.sum(jnp.exp(logits - local_max[:, None, :]), axis=1)
    joined = exchange(jnp.stack([local_max, local_total]), ("col",), join_softmax, 1)
    probs = jnp.exp(logits - joined[0][:, None, :]) / joined[1][:, None, :]
    probs_low = probs.astype(jnp.bfloat16)
    probs_low = jnp.concatenate([probs_low, lax.ppermute(probs_low, "col", partners)], axis=1)

    v = jnp.dot(everyone.reshape(-1, width), entries, preferred_element_type=jnp.float32)
    v = v.astype(jnp.bfloat16).reshape(blocks // 2, strands, 2 * tokens, heads, head_width)
    v = v.transpose(3, 2, 0, 1, 4).reshape(heads, 2 * tokens, blocks // 2 * lanes)
    f = everyone.transpose(1, 3, 0, 2).reshape(strands * width, blocks * tokens)

    d_own, d_other = d_probs_of(g, v)
    d_probs = d_own + lax.ppermute(d_other, "col", partners).astype(jnp.float32)
    crossed = value_weight_of(g, probs_low, f, strands)
    row_dot = exchange(jnp.sum(probs * d_probs, axis=1), ("col",), add_up, 2)
    d_logits = (probs * (d_probs - row_dot[:, None, :])).astype(jnp.bfloat16)
    d_pair, d_pair_weight = pair_gradients(
        d_logits.transpose(0, 2, 1).reshape(heads, rows * tokens),
        pair.reshape(rows * tokens, pair_width), pair_weight.T)
    d_value_weight = crossed.reshape(width, heads, strands, head_width).sum(2)
    both = jnp.concatenate([d_pair_weight.reshape(-1), d_value_weight.reshape(-1)]).reshape(-1, 128)
    both = exchange(both, ("row",), add_up, 3)
    both = exchange(both, ("col",), add_up, 4).reshape(-1)
    both = both * (1.0 / token_total)
    cut = heads * pair_width
    return (
        d_pair.reshape(pair.shape),
        both[:cut].reshape(heads, pair_width).T,
        both[cut:].reshape(width, width),
    )


def solution(mesh):
    placed = (P("row", "col", None), P(), P("row", "col", None), P("col", "row", None), P())
    return jax.shard_map(
        on_device,
        mesh=mesh,
        in_specs=placed,
        out_specs=(P("row", "col", None), P(), P()),
        check_vma=False,
    )
```

```python
import functools
import math

import jax
import jax.numpy as jnp
from jax import lax
from jax.experimental import pallas as pl
from jax.experimental.pallas import tpu as pltpu
from jax.sharding import PartitionSpec as P

MESH = pl.DeviceIdType.MESH
VMEM_BYTES = 48 * 1024 * 1024


def exchange_kernel(axes, combine, mine, out, slots, send, recv):
    sizes = [lax.axis_size(a) for a in axes]
    n = math.prod(sizes)
    me = lax.axis_index(axes[0])
    for a, size in zip(axes[1:], sizes[1:]):
        me = me * size + lax.axis_index(a)

    def device(p):
        if len(axes) == 1:
            return {axes[0]: p}
        return {axes[0]: p // sizes[1], axes[1]: p % sizes[1]}

    barrier = pltpu.get_barrier_semaphore()

    def greet(d, carry):
        pl.semaphore_signal(barrier, inc=1, device_id=device(lax.rem(me + d, n)), device_id_type=MESH)
        return carry

    lax.fori_loop(1, n, greet, 0)
    pl.semaphore_wait(barrier, n - 1)

    def copy(to, slot):
        return pltpu.make_async_remote_copy(
            src_ref=mine, dst_ref=slots.at[slot], send_sem=send.at[to], recv_sem=recv.at[slot],
            device_id=device(to), device_id_type=MESH)

    def begin(d, carry):
        copy(lax.rem(me + d, n), me).start()
        return carry

    lax.fori_loop(1, n, begin, 0)
    slots[me] = mine[...]

    def finish(d, carry):
        peer = lax.rem(me + d, n)
        copy(peer, peer).wait_recv()
        copy(peer, me).wait_send()
        return carry

    lax.fori_loop(1, n, finish, 0)
    combine(n, slots, out)


def add_up(n, slots, out):
    out[...] = lax.fori_loop(1, n, lambda p, total: total + slots[p], slots[0])


def join_softmax(n, slots, out):
    top = lax.fori_loop(1, n, lambda p, m: jnp.maximum(m, slots[p, 0]), slots[0, 0])
    total = lax.fori_loop(
        0, n, lambda p, t: t + slots[p, 1] * jnp.exp(slots[p, 0] - top), jnp.zeros_like(top))
    out[0] = top
    out[1] = total


def exchange(x, axes, combine, collective_id):
    n = math.prod(lax.axis_size(a) for a in axes)
    return pl.pallas_call(
        functools.partial(exchange_kernel, axes, combine),
        out_shape=jax.ShapeDtypeStruct(x.shape, x.dtype),
        in_specs=[pl.BlockSpec(memory_space=pltpu.VMEM)],
        out_specs=pl.BlockSpec(memory_space=pltpu.VMEM),
        scratch_shapes=[
            pltpu.VMEM((n,) + x.shape, x.dtype),
            pltpu.SemaphoreType.DMA((n,)),
            pltpu.SemaphoreType.DMA((n,)),
        ],
        compiler_params=pltpu.CompilerParams(
            collective_id=collective_id, has_side_effects=True, vmem_limit_bytes=VMEM_BYTES),
    )(x)


def d_probs_kernel(heads, own, g, v, d_own, d_other, total):
    step = pl.program_id(0)

    @pl.when(step == 0)
    def _():
        total[...] = jnp.zeros_like(total)

    for h in range(heads):
        total[h] += lax.dot_general(
            v[h], g[0, h], (((1,), (1,)), ((), ())), preferred_element_type=jnp.float32)

    @pl.when(step == pl.num_programs(0) - 1)
    def _():
        d_own[...] = total[:, :own]
        d_other[...] = total[:, own:].astype(jnp.bfloat16)


def whole(shape):
    return pl.BlockSpec(shape, lambda c: (0,) * len(shape))


def d_probs_of(g, v):
    steps, heads, rows, lanes = g.shape
    tokens = v.shape[1]
    half = (heads, tokens // 2, rows)
    return pl.pallas_call(
        functools.partial(d_probs_kernel, heads, tokens // 2),
        grid=(steps,),
        in_specs=[
            pl.BlockSpec((1, heads, rows, lanes), lambda c: (c, 0, 0, 0)),
            pl.BlockSpec((heads, tokens, lanes), lambda c: (0, 0, c)),
        ],
        out_specs=[whole(half), whole(half)],
        out_shape=[jax.ShapeDtypeStruct(half, jnp.float32), jax.ShapeDtypeStruct(half, jnp.bfloat16)],
        scratch_shapes=[pltpu.VMEM((heads, tokens, rows), jnp.float32)],
        compiler_params=pltpu.CompilerParams(vmem_limit_bytes=VMEM_BYTES),
        cost_estimate=pl.CostEstimate(
            flops=2 * g.size * tokens, bytes_accessed=2 * g.size, transcendentals=0),
    )(g, v)


def value_kernel(heads, strands, g, p, f, weight, d_values):
    step = pl.program_id(0)
    tokens, lanes = p.shape[1], g.shape[3]
    rows = pl.ds(pl.multiple_of(step * tokens, tokens), tokens)
    for h in range(heads):
        d_values[rows, h * lanes:(h + 1) * lanes] = jnp.dot(
            p[h], g[0, h], preferred_element_type=jnp.float32).astype(jnp.bfloat16)

    @pl.when(step == pl.num_programs(0) - 1)
    def _():
        width = f.shape[0] // strands
        head_width = lanes // strands
        strand_of_lane = (lax.broadcasted_iota(jnp.int32, (width, heads * lanes), 1) % lanes) // head_width
        part = strands // 4
        total = jnp.zeros((width, heads * lanes), jnp.float32)
        for q in range(4):
            cross = jnp.dot(
                f[q * part * width:(q + 1) * part * width, :], d_values[...],
                preferred_element_type=jnp.float32)
            for s in range(part):
                total += jnp.where(
                    strand_of_lane == q * part + s, cross[s * width:(s + 1) * width], 0.0)
        weight[...] = total


def value_weight_of(g, p, f, strands):
    steps, heads, rows, lanes = g.shape
    tokens = p.shape[1]
    width = f.shape[0] // strands
    return pl.pallas_call(
        functools.partial(value_kernel, heads, strands),
        grid=(steps,),
        in_specs=[
            pl.BlockSpec((1, heads, rows, lanes), lambda c: (c, 0, 0, 0)),
            whole(p.shape),
            whole(f.shape),
        ],
        out_specs=whole((width, heads * lanes)),
        out_shape=jax.ShapeDtypeStruct((width, heads * lanes), jnp.float32),
        scratch_shapes=[pltpu.VMEM((steps * tokens, heads * lanes), jnp.bfloat16)],
        compiler_params=pltpu.CompilerParams(vmem_limit_bytes=VMEM_BYTES),
        cost_estimate=pl.CostEstimate(
            flops=4 * g.size * tokens, bytes_accessed=2 * g.size, transcendentals=0),
    )(g, p, f)


def pair_kernel(d_logits, pair, weight, d_pair, d_weight):
    @pl.when(pl.program_id(0) == 0)
    def _():
        d_weight[...] = jnp.zeros_like(d_weight)

    d_pair[...] = lax.dot_general(
        d_logits[...], weight[...], (((0,), (0,)), ((), ())), preferred_element_type=jnp.float32
    ).astype(jnp.bfloat16)
    d_weight[...] += jnp.dot(d_logits[...], pair[...], preferred_element_type=jnp.float32)


def pair_gradients(d_logits, pair, weight):
    heads, cells = d_logits.shape
    width = pair.shape[1]
    block = 4096
    return pl.pallas_call(
        pair_kernel,
        grid=(cells // block,),
        in_specs=[
            pl.BlockSpec((heads, block), lambda c: (0, c)),
            pl.BlockSpec((block, width), lambda c: (c, 0)),
            whole((heads, width)),
        ],
        out_specs=[pl.BlockSpec((block, width), lambda c: (c, 0)), whole((heads, width))],
        out_shape=[
            jax.ShapeDtypeStruct((cells, width), jnp.bfloat16),
            jax.ShapeDtypeStruct((heads, width), jnp.float32),
        ],
        compiler_params=pltpu.CompilerParams(vmem_limit_bytes=VMEM_BYTES),
    )(d_logits, pair, weight)


def on_device(pair, pair_weight, features, sensitivity, entries):
    rows, tokens, pair_width = pair.shape
    heads = pair_weight.shape[1]
    strands, _, width = sensitivity.shape
    head_width = width // heads
    blocks = lax.axis_size("col")
    token_total = tokens * blocks
    lanes = strands * head_width
    parity = lax.axis_index("col") % 2
    groups = [list(range(q, blocks, 2)) for q in range(2)]
    partners = [(c, c ^ 1) for c in range(blocks)]

    g = sensitivity.reshape(strands, rows, heads, head_width)
    g = g.transpose(2, 1, 0, 3).reshape(heads, rows, lanes)
    g, features, pair = lax.optimization_barrier((g, features, pair))
    g = lax.all_gather(g, "col", axis=0, axis_index_groups=groups)

    features = features.reshape(-1, 2, strands, tokens, width)
    kept = lax.dynamic_index_in_dim(features, parity, 1, keepdims=False)
    sent = lax.dynamic_index_in_dim(features, 1 - parity, 1, keepdims=False)
    both_tokens = jnp.concatenate([kept, lax.ppermute(sent, "col", partners)], axis=2)
    row, row_count = lax.axis_index("row"), lax.axis_size("row")
    everyone = jnp.zeros((row_count,) + both_tokens.shape, both_tokens.dtype)
    for d in range(row_count):
        part = both_tokens
        if d:
            part = lax.ppermute(part, "row", [(r, (r + d) % row_count) for r in range(row_count)])
        everyone = lax.dynamic_update_index_in_dim(everyone, part, (row - d) % row_count, 0)
    everyone = everyone.reshape((-1,) + both_tokens.shape[1:])
    logits = jnp.einsum("ijk,kh->hji", pair, pair_weight, preferred_element_type=jnp.float32)
    local_max = jnp.max(logits, axis=1)
    local_total = jnp.sum(jnp.exp(logits - local_max[:, None, :]), axis=1)
    joined = exchange(jnp.stack([local_max, local_total]), ("col",), join_softmax, 1)
    probs = jnp.exp(logits - joined[0][:, None, :]) / joined[1][:, None, :]
    probs_low = probs.astype(jnp.bfloat16)
    probs_low = jnp.concatenate([probs_low, lax.ppermute(probs_low, "col", partners)], axis=1)

    v = jnp.dot(everyone.reshape(-1, width), entries, preferred_element_type=jnp.float32)
    v = v.astype(jnp.bfloat16).reshape(blocks // 2, strands, 2 * tokens, heads, head_width)
    v = v.transpose(3, 2, 0, 1, 4).reshape(heads, 2 * tokens, blocks // 2 * lanes)
    f = everyone.transpose(1, 3, 0, 2).reshape(strands * width, blocks * tokens)

    g, v, f, probs, probs_low = lax.optimization_barrier((g, v, f, probs, probs_low))
    d_own, d_other = d_probs_of(g, v)
    d_probs = d_own + lax.ppermute(d_other, "col", partners).astype(jnp.float32)
    crossed = value_weight_of(g, probs_low, f, strands)
    row_dot = exchange(jnp.sum(probs * d_probs, axis=1), ("col",), add_up, 2)
    d_logits = (probs * (d_probs - row_dot[:, None, :])).astype(jnp.bfloat16)
    d_pair, d_pair_weight = pair_gradients(
        d_logits.transpose(0, 2, 1).reshape(heads, rows * tokens),
        pair.reshape(rows * tokens, pair_width), pair_weight.T)
    d_value_weight = crossed.reshape(width, heads, strands, head_width).sum(2)
    both = jnp.concatenate([d_pair_weight.reshape(-1), d_value_weight.reshape(-1)]).reshape(-1, 128)
    both = exchange(both, ("row",), add_up, 3)
    both = exchange(both, ("col",), add_up, 4).reshape(-1)
    both = both * (1.0 / token_total)
    cut = heads * pair_width
    return (
        d_pair.reshape(pair.shape),
        both[:cut].reshape(heads, pair_width).T,
        both[cut:].reshape(width, width),
    )


def solution(mesh):
    placed = (P("row", "col", None), P(), P("row", "col", None), P("col", "row", None), P())
    return jax.shard_map(
        on_device,
        mesh=mesh,
        in_specs=placed,
        out_specs=(P("row", "col", None), P(), P()),
        check_vma=False,
    )
```

```python
import functools
import math

import jax
import jax.numpy as jnp
from jax import lax
from jax.experimental import pallas as pl
from jax.experimental.pallas import tpu as pltpu
from jax.sharding import PartitionSpec as P

MESH = pl.DeviceIdType.MESH
VMEM_BYTES = 48 * 1024 * 1024


def exchange_kernel(axes, combine, mine, out, slots, send, recv):
    sizes = [lax.axis_size(a) for a in axes]
    n = math.prod(sizes)
    me = lax.axis_index(axes[0])
    for a, size in zip(axes[1:], sizes[1:]):
        me = me * size + lax.axis_index(a)

    def device(p):
        if len(axes) == 1:
            return {axes[0]: p}
        return {axes[0]: p // sizes[1], axes[1]: p % sizes[1]}

    barrier = pltpu.get_barrier_semaphore()

    def greet(d, carry):
        pl.semaphore_signal(barrier, inc=1, device_id=device(lax.rem(me + d, n)), device_id_type=MESH)
        return carry

    lax.fori_loop(1, n, greet, 0)
    pl.semaphore_wait(barrier, n - 1)

    def copy(to, slot):
        return pltpu.make_async_remote_copy(
            src_ref=mine, dst_ref=slots.at[slot], send_sem=send.at[to], recv_sem=recv.at[slot],
            device_id=device(to), device_id_type=MESH)

    def begin(d, carry):
        copy(lax.rem(me + d, n), me).start()
        return carry

    lax.fori_loop(1, n, begin, 0)
    slots[me] = mine[...]

    def finish(d, carry):
        peer = lax.rem(me + d, n)
        copy(peer, peer).wait_recv()
        copy(peer, me).wait_send()
        return carry

    lax.fori_loop(1, n, finish, 0)
    combine(n, slots, out)


def add_up(n, slots, out):
    out[...] = lax.fori_loop(1, n, lambda p, total: total + slots[p], slots[0])


def join_softmax(n, slots, out):
    top = lax.fori_loop(1, n, lambda p, m: jnp.maximum(m, slots[p, 0]), slots[0, 0])
    total = lax.fori_loop(
        0, n, lambda p, t: t + slots[p, 1] * jnp.exp(slots[p, 0] - top), jnp.zeros_like(top))
    out[0] = top
    out[1] = total


def exchange(x, axes, combine, collective_id):
    n = math.prod(lax.axis_size(a) for a in axes)
    return pl.pallas_call(
        functools.partial(exchange_kernel, axes, combine),
        out_shape=jax.ShapeDtypeStruct(x.shape, x.dtype),
        in_specs=[pl.BlockSpec(memory_space=pltpu.VMEM)],
        out_specs=pl.BlockSpec(memory_space=pltpu.VMEM),
        scratch_shapes=[
            pltpu.VMEM((n,) + x.shape, x.dtype),
            pltpu.SemaphoreType.DMA((n,)),
            pltpu.SemaphoreType.DMA((n,)),
        ],
        compiler_params=pltpu.CompilerParams(
            collective_id=collective_id, has_side_effects=True, vmem_limit_bytes=VMEM_BYTES),
    )(x)


def d_probs_kernel(heads, own, g, v, d_own, *rest):
    d_others, total = rest[:-1], rest[-1]
    step = pl.program_id(0)

    @pl.when(step == 0)
    def _():
        total[...] = jnp.zeros_like(total)

    for h in range(heads):
        total[h] += lax.dot_general(
            v[h], g[0, h], (((1,), (1,)), ((), ())), preferred_element_type=jnp.float32)

    @pl.when(step == pl.num_programs(0) - 1)
    def _():
        d_own[...] = total[:, :own]
        for d, other in enumerate(d_others, 1):
            other[...] = total[:, d * own:(d + 1) * own].astype(jnp.bfloat16)


def whole(shape):
    return pl.BlockSpec(shape, lambda c: (0,) * len(shape))


def d_probs_of(g, v, group):
    steps, heads, rows, lanes = g.shape
    tokens = v.shape[1]
    share = (heads, tokens // group, rows)
    return pl.pallas_call(
        functools.partial(d_probs_kernel, heads, tokens // group),
        grid=(steps,),
        in_specs=[
            pl.BlockSpec((1, heads, rows, lanes), lambda c: (c, 0, 0, 0)),
            pl.BlockSpec((heads, tokens, lanes), lambda c: (0, 0, c)),
        ],
        out_specs=[whole(share)] * group,
        out_shape=[jax.ShapeDtypeStruct(share, jnp.float32)]
        + [jax.ShapeDtypeStruct(share, jnp.bfloat16)] * (group - 1),
        scratch_shapes=[pltpu.VMEM((heads, tokens, rows), jnp.float32)],
        compiler_params=pltpu.CompilerParams(vmem_limit_bytes=VMEM_BYTES),
        cost_estimate=pl.CostEstimate(
            flops=2 * g.size * tokens, bytes_accessed=2 * g.size, transcendentals=0),
    )(g, v)


def value_kernel(heads, strands, g, p, f, weight, d_values):
    step = pl.program_id(0)
    tokens, lanes = p.shape[1], g.shape[3]
    rows = pl.ds(pl.multiple_of(step * tokens, tokens), tokens)
    for h in range(heads):
        d_values[rows, h * lanes:(h + 1) * lanes] = jnp.dot(
            p[h], g[0, h], preferred_element_type=jnp.float32).astype(jnp.bfloat16)

    @pl.when(step == pl.num_programs(0) - 1)
    def _():
        width = f.shape[0] // strands
        head_width = lanes // strands
        strand_of_lane = (lax.broadcasted_iota(jnp.int32, (width, heads * lanes), 1) % lanes) // head_width
        part = strands // 4
        total = jnp.zeros((width, heads * lanes), jnp.float32)
        for q in range(4):
            cross = jnp.dot(
                f[q * part * width:(q + 1) * part * width, :], d_values[...],
                preferred_element_type=jnp.float32)
            for s in range(part):
                total += jnp.where(
                    strand_of_lane == q * part + s, cross[s * width:(s + 1) * width], 0.0)
        weight[...] = total


def value_weight_of(g, p, f, strands):
    steps, heads, rows, lanes = g.shape
    tokens = p.shape[1]
    width = f.shape[0] // strands
    return pl.pallas_call(
        functools.partial(value_kernel, heads, strands),
        grid=(steps,),
        in_specs=[
            pl.BlockSpec((1, heads, rows, lanes), lambda c: (c, 0, 0, 0)),
            whole(p.shape),
            whole(f.shape),
        ],
        out_specs=whole((width, heads * lanes)),
        out_shape=jax.ShapeDtypeStruct((width, heads * lanes), jnp.float32),
        scratch_shapes=[pltpu.VMEM((steps * tokens, heads * lanes), jnp.bfloat16)],
        compiler_params=pltpu.CompilerParams(vmem_limit_bytes=VMEM_BYTES),
        cost_estimate=pl.CostEstimate(
            flops=4 * g.size * tokens, bytes_accessed=2 * g.size, transcendentals=0),
    )(g, p, f)


def pair_kernel(d_logits, pair, weight, d_pair, d_weight):
    @pl.when(pl.program_id(0) == 0)
    def _():
        d_weight[...] = jnp.zeros_like(d_weight)

    d_pair[...] = lax.dot_general(
        d_logits[...], weight[...], (((0,), (0,)), ((), ())), preferred_element_type=jnp.float32
    ).astype(jnp.bfloat16)
    d_weight[...] += jnp.dot(d_logits[...], pair[...], preferred_element_type=jnp.float32)


def pair_gradients(d_logits, pair, weight):
    heads, cells = d_logits.shape
    width = pair.shape[1]
    block = 4096
    return pl.pallas_call(
        pair_kernel,
        grid=(cells // block,),
        in_specs=[
            pl.BlockSpec((heads, block), lambda c: (0, c)),
            pl.BlockSpec((block, width), lambda c: (c, 0)),
            whole((heads, width)),
        ],
        out_specs=[pl.BlockSpec((block, width), lambda c: (c, 0)), whole((heads, width))],
        out_shape=[
            jax.ShapeDtypeStruct((cells, width), jnp.bfloat16),
            jax.ShapeDtypeStruct((heads, width), jnp.float32),
        ],
        compiler_params=pltpu.CompilerParams(vmem_limit_bytes=VMEM_BYTES),
    )(d_logits, pair, weight)


def on_device(pair, pair_weight, features, sensitivity, entries):
    rows, tokens, pair_width = pair.shape
    heads = pair_weight.shape[1]
    strands, _, width = sensitivity.shape
    head_width = width // heads
    blocks = lax.axis_size("col")
    token_total = tokens * blocks
    lanes = strands * head_width
    group = math.gcd(4, features.shape[0] // strands)
    place = lax.axis_index("col") % group
    groups = [list(range(q, blocks, group)) for q in range(group)]

    def swap(x, d):
        return lax.ppermute(x, "col", [(c, c ^ d) for c in range(blocks)])


    g = sensitivity.reshape(strands, rows, heads, head_width)
    g = g.transpose(2, 1, 0, 3).reshape(heads, rows, lanes)
    g, features, pair = lax.optimization_barrier((g, features, pair))
    g = lax.all_gather(g, "col", axis=0, axis_index_groups=groups)

    features = features.reshape(-1, group, strands, tokens, width)
    shares = [lax.dynamic_index_in_dim(features, place ^ d, 1, keepdims=False) for d in range(group)]
    shares = shares[:1] + [swap(share, d) for d, share in enumerate(shares[1:], 1)]
    group_tokens = jnp.concatenate(shares, axis=2)
    row, row_count = lax.axis_index("row"), lax.axis_size("row")
    everyone = jnp.zeros((row_count,) + group_tokens.shape, group_tokens.dtype)
    for d in range(row_count):
        part = group_tokens
        if d:
            part = lax.ppermute(part, "row", [(r, (r + d) % row_count) for r in range(row_count)])
        everyone = lax.dynamic_update_index_in_dim(everyone, part, (row - d) % row_count, 0)
    everyone = everyone.reshape((-1,) + group_tokens.shape[1:])
    logits = jnp.einsum("ijk,kh->hji", pair, pair_weight, preferred_element_type=jnp.float32)
    local_max = jnp.max(logits, axis=1)
    local_total = jnp.sum(jnp.exp(logits - local_max[:, None, :]), axis=1)
    joined = exchange(jnp.stack([local_max, local_total]), ("col",), join_softmax, 1)
    probs = jnp.exp(logits - joined[0][:, None, :]) / joined[1][:, None, :]
    probs_low = probs.astype(jnp.bfloat16)
    probs_low = jnp.concatenate([probs_low] + [swap(probs_low, d) for d in range(1, group)], axis=1)

    v = jnp.dot(everyone.reshape(-1, width), entries, preferred_element_type=jnp.float32)
    v = v.astype(jnp.bfloat16).reshape(blocks // group, strands, group * tokens, heads, head_width)
    v = v.transpose(3, 2, 0, 1, 4).reshape(heads, group * tokens, blocks // group * lanes)
    f = everyone.transpose(1, 3, 0, 2).reshape(strands * width, blocks * tokens)

    g, v, f, probs, probs_low = lax.optimization_barrier((g, v, f, probs, probs_low))
    d_probs, *d_others = d_probs_of(g, v, group)
    for d, other in enumerate(d_others, 1):
        d_probs += swap(other, d).astype(jnp.float32)
    crossed = value_weight_of(g, probs_low, f, strands)
    row_dot = exchange(jnp.sum(probs * d_probs, axis=1), ("col",), add_up, 2)
    d_logits = (probs * (d_probs - row_dot[:, None, :])).astype(jnp.bfloat16)
    d_pair, d_pair_weight = pair_gradients(
        d_logits.transpose(0, 2, 1).reshape(heads, rows * tokens),
        pair.reshape(rows * tokens, pair_width), pair_weight.T)
    d_value_weight = crossed.reshape(width, heads, strands, head_width).sum(2)
    both = jnp.concatenate([d_pair_weight.reshape(-1), d_value_weight.reshape(-1)]).reshape(-1, 128)
    both = exchange(both, ("row",), add_up, 3)
    both = exchange(both, ("col",), add_up, 4).reshape(-1)
    both = both * (1.0 / token_total)
    cut = heads * pair_width
    return (
        d_pair.reshape(pair.shape),
        both[:cut].reshape(heads, pair_width).T,
        both[cut:].reshape(width, width),
    )


def solution(mesh):
    placed = (P("row", "col", None), P(), P("row", "col", None), P("col", "row", None), P())
    return jax.shard_map(
        on_device,
        mesh=mesh,
        in_specs=placed,
        out_specs=(P("row", "col", None), P(), P()),
        check_vma=False,
    )
```

```python
import functools
import math

import jax
import jax.numpy as jnp
from jax import lax
from jax.experimental import pallas as pl
from jax.experimental.pallas import tpu as pltpu
from jax.sharding import PartitionSpec as P

MESH = pl.DeviceIdType.MESH
VMEM_BYTES = 48 * 1024 * 1024


def exchange_kernel(axes, combine, mine, out, slots, send, recv):
    sizes = [lax.axis_size(a) for a in axes]
    n = math.prod(sizes)
    me = lax.axis_index(axes[0])
    for a, size in zip(axes[1:], sizes[1:]):
        me = me * size + lax.axis_index(a)

    def device(p):
        if len(axes) == 1:
            return {axes[0]: p}
        return {axes[0]: p // sizes[1], axes[1]: p % sizes[1]}

    barrier = pltpu.get_barrier_semaphore()

    def greet(d, carry):
        pl.semaphore_signal(barrier, inc=1, device_id=device(lax.rem(me + d, n)), device_id_type=MESH)
        return carry

    lax.fori_loop(1, n, greet, 0)
    pl.semaphore_wait(barrier, n - 1)

    def copy(to, slot):
        return pltpu.make_async_remote_copy(
            src_ref=mine, dst_ref=slots.at[slot], send_sem=send.at[to], recv_sem=recv.at[slot],
            device_id=device(to), device_id_type=MESH)

    def begin(d, carry):
        copy(lax.rem(me + d, n), me).start()
        return carry

    lax.fori_loop(1, n, begin, 0)
    slots[me] = mine[...]

    def finish(d, carry):
        peer = lax.rem(me + d, n)
        copy(peer, peer).wait_recv()
        copy(peer, me).wait_send()
        return carry

    lax.fori_loop(1, n, finish, 0)
    combine(n, slots, out)


def add_up(n, slots, out):
    out[...] = lax.fori_loop(1, n, lambda p, total: total + slots[p], slots[0])


def join_softmax(n, slots, out):
    top = lax.fori_loop(1, n, lambda p, m: jnp.maximum(m, slots[p, 0]), slots[0, 0])
    total = lax.fori_loop(
        0, n, lambda p, t: t + slots[p, 1] * jnp.exp(slots[p, 0] - top), jnp.zeros_like(top))
    out[0] = top
    out[1] = total


def exchange(x, axes, combine, collective_id):
    n = math.prod(lax.axis_size(a) for a in axes)
    return pl.pallas_call(
        functools.partial(exchange_kernel, axes, combine),
        out_shape=jax.ShapeDtypeStruct(x.shape, x.dtype),
        in_specs=[pl.BlockSpec(memory_space=pltpu.VMEM)],
        out_specs=pl.BlockSpec(memory_space=pltpu.VMEM),
        scratch_shapes=[
            pltpu.VMEM((n,) + x.shape, x.dtype),
            pltpu.SemaphoreType.DMA((n,)),
            pltpu.SemaphoreType.DMA((n,)),
        ],
        compiler_params=pltpu.CompilerParams(
            collective_id=collective_id, has_side_effects=True, vmem_limit_bytes=VMEM_BYTES),
    )(x)


def d_probs_kernel(heads, own, g, v, d_own, *rest):
    d_others, total = rest[:-1], rest[-1]
    step = pl.program_id(0)

    @pl.when(step == 0)
    def _():
        total[...] = jnp.zeros_like(total)

    for h in range(heads):
        total[h] += lax.dot_general(
            v[h], g[0, h], (((1,), (1,)), ((), ())), preferred_element_type=jnp.float32)

    @pl.when(step == pl.num_programs(0) - 1)
    def _():
        d_own[...] = total[:, :own]
        for d, other in enumerate(d_others, 1):
            other[...] = total[:, d * own:(d + 1) * own].astype(jnp.bfloat16)


def whole(shape):
    return pl.BlockSpec(shape, lambda c: (0,) * len(shape))


def d_probs_of(g, v, group):
    steps, heads, rows, lanes = g.shape
    tokens = v.shape[1]
    share = (heads, tokens // group, rows)
    return pl.pallas_call(
        functools.partial(d_probs_kernel, heads, tokens // group),
        grid=(steps,),
        in_specs=[
            pl.BlockSpec((1, heads, rows, lanes), lambda c: (c, 0, 0, 0)),
            pl.BlockSpec((heads, tokens, lanes), lambda c: (0, 0, c)),
        ],
        out_specs=[whole(share)] * group,
        out_shape=[jax.ShapeDtypeStruct(share, jnp.float32)]
        + [jax.ShapeDtypeStruct(share, jnp.bfloat16)] * (group - 1),
        scratch_shapes=[pltpu.VMEM((heads, tokens, rows), jnp.float32)],
        compiler_params=pltpu.CompilerParams(vmem_limit_bytes=VMEM_BYTES),
        cost_estimate=pl.CostEstimate(
            flops=2 * g.size * tokens, bytes_accessed=2 * g.size, transcendentals=0),
    )(g, v)


def value_kernel(heads, strands, g, p, f, weight, d_values):
    step = pl.program_id(0)
    tokens, lanes = p.shape[1], g.shape[3]
    rows = pl.ds(pl.multiple_of(step * tokens, tokens), tokens)
    for h in range(heads):
        d_values[rows, h * lanes:(h + 1) * lanes] = jnp.dot(
            p[h], g[0, h], preferred_element_type=jnp.float32).astype(jnp.bfloat16)

    @pl.when(step == pl.num_programs(0) - 1)
    def _():
        width = f.shape[0] // strands
        head_width = lanes // strands
        strand_of_lane = (lax.broadcasted_iota(jnp.int32, (width, heads * lanes), 1) % lanes) // head_width
        part = strands // 4
        total = jnp.zeros((width, heads * lanes), jnp.float32)
        for q in range(4):
            cross = jnp.dot(
                f[q * part * width:(q + 1) * part * width, :], d_values[...],
                preferred_element_type=jnp.float32)
            for s in range(part):
                total += jnp.where(
                    strand_of_lane == q * part + s, cross[s * width:(s + 1) * width], 0.0)
        weight[...] = total


def value_weight_of(g, p, f, strands):
    steps, heads, rows, lanes = g.shape
    tokens = p.shape[1]
    width = f.shape[0] // strands
    return pl.pallas_call(
        functools.partial(value_kernel, heads, strands),
        grid=(steps,),
        in_specs=[
            pl.BlockSpec((1, heads, rows, lanes), lambda c: (c, 0, 0, 0)),
            whole(p.shape),
            whole(f.shape),
        ],
        out_specs=whole((width, heads * lanes)),
        out_shape=jax.ShapeDtypeStruct((width, heads * lanes), jnp.float32),
        scratch_shapes=[pltpu.VMEM((steps * tokens, heads * lanes), jnp.bfloat16)],
        compiler_params=pltpu.CompilerParams(vmem_limit_bytes=VMEM_BYTES),
        cost_estimate=pl.CostEstimate(
            flops=4 * g.size * tokens, bytes_accessed=2 * g.size, transcendentals=0),
    )(g, p, f)


def pair_kernel(d_logits, pair, weight, d_pair, d_weight):
    @pl.when(pl.program_id(0) == 0)
    def _():
        d_weight[...] = jnp.zeros_like(d_weight)

    d_pair[...] = lax.dot_general(
        d_logits[...], weight[...], (((0,), (0,)), ((), ())), preferred_element_type=jnp.float32
    ).astype(jnp.bfloat16)
    d_weight[...] += jnp.dot(d_logits[...], pair[...], preferred_element_type=jnp.float32)


def pair_gradients(d_logits, pair, weight):
    heads, cells = d_logits.shape
    width = pair.shape[1]
    block = 4096
    return pl.pallas_call(
        pair_kernel,
        grid=(cells // block,),
        in_specs=[
            pl.BlockSpec((heads, block), lambda c: (0, c)),
            pl.BlockSpec((block, width), lambda c: (c, 0)),
            whole((heads, width)),
        ],
        out_specs=[pl.BlockSpec((block, width), lambda c: (c, 0)), whole((heads, width))],
        out_shape=[
            jax.ShapeDtypeStruct((cells, width), jnp.bfloat16),
            jax.ShapeDtypeStruct((heads, width), jnp.float32),
        ],
        compiler_params=pltpu.CompilerParams(vmem_limit_bytes=VMEM_BYTES),
    )(d_logits, pair, weight)


def on_device(pair, pair_weight, features, sensitivity, entries):
    rows, tokens, pair_width = pair.shape
    heads = pair_weight.shape[1]
    strands, _, width = sensitivity.shape
    head_width = width // heads
    blocks = lax.axis_size("col")
    token_total = tokens * blocks
    lanes = strands * head_width
    group = math.gcd(4, features.shape[0] // strands)
    place = lax.axis_index("col") % group
    groups = [list(range(q, blocks, group)) for q in range(group)]

    def swap(x, d):
        return lax.ppermute(x, "col", [(c, c ^ d) for c in range(blocks)])


    g = sensitivity.reshape(strands, rows, heads, head_width)
    g = g.transpose(2, 1, 0, 3).reshape(heads, rows, lanes)
    g, features, pair = lax.optimization_barrier((g, features, pair))
    g = lax.all_gather(g, "col", axis=0, axis_index_groups=groups)

    features = features.reshape(-1, group, strands, tokens, width)
    shares = [lax.dynamic_index_in_dim(features, place ^ d, 1, keepdims=False) for d in range(group)]
    shares = shares[:1] + [swap(share, d) for d, share in enumerate(shares[1:], 1)]
    group_tokens = jnp.concatenate(shares, axis=2)
    row, row_count = lax.axis_index("row"), lax.axis_size("row")
    everyone = jnp.zeros((row_count,) + group_tokens.shape, group_tokens.dtype)
    for d in range(row_count):
        part = group_tokens
        if d:
            part = lax.ppermute(part, "row", [(r, (r + d) % row_count) for r in range(row_count)])
        everyone = lax.dynamic_update_index_in_dim(everyone, part, (row - d) % row_count, 0)
    everyone = everyone.reshape((-1,) + group_tokens.shape[1:])
    logits = jnp.einsum("ijk,kh->hji", pair, pair_weight, preferred_element_type=jnp.float32)
    local_max = jnp.max(logits, axis=1)
    local_total = jnp.sum(jnp.exp(logits - local_max[:, None, :]), axis=1)
    joined = exchange(jnp.stack([local_max, local_total]), ("col",), join_softmax, 1)
    probs = jnp.exp(logits - joined[0][:, None, :]) / joined[1][:, None, :]
    probs_low = probs.astype(jnp.bfloat16)
    probs_low = jnp.concatenate([probs_low] + [swap(probs_low, d) for d in range(1, group)], axis=1)

    v = jnp.dot(everyone.reshape(-1, width), entries, preferred_element_type=jnp.float32)
    v = v.astype(jnp.bfloat16).reshape(blocks // group, strands, group * tokens, heads, head_width)
    v = v.transpose(3, 2, 0, 1, 4).reshape(heads, group * tokens, blocks // group * lanes)
    f = everyone.transpose(1, 3, 0, 2).reshape(strands * width, blocks * tokens)

    g, v, probs = lax.optimization_barrier((g, v, probs))
    d_probs, *d_others = d_probs_of(g, v, group)
    for d, other in enumerate(d_others, 1):
        d_probs += swap(other, d).astype(jnp.float32)
    crossed = value_weight_of(g, probs_low, f, strands)
    row_dot = exchange(jnp.sum(probs * d_probs, axis=1), ("col",), add_up, 2)
    d_logits = (probs * (d_probs - row_dot[:, None, :])).astype(jnp.bfloat16)
    d_pair, d_pair_weight = pair_gradients(
        d_logits.transpose(0, 2, 1).reshape(heads, rows * tokens),
        pair.reshape(rows * tokens, pair_width), pair_weight.T)
    d_value_weight = crossed.reshape(width, heads, strands, head_width).sum(2)
    both = jnp.concatenate([d_pair_weight.reshape(-1), d_value_weight.reshape(-1)]).reshape(-1, 128)
    both = exchange(both, ("row",), add_up, 3)
    both = exchange(both, ("col",), add_up, 4).reshape(-1)
    both = both * (1.0 / token_total)
    cut = heads * pair_width
    return (
        d_pair.reshape(pair.shape),
        both[:cut].reshape(heads, pair_width).T,
        both[cut:].reshape(width, width),
    )


def solution(mesh):
    placed = (P("row", "col", None), P(), P("row", "col", None), P("col", "row", None), P())
    return jax.shard_map(
        on_device,
        mesh=mesh,
        in_specs=placed,
        out_specs=(P("row", "col", None), P(), P()),
        check_vma=False,
    )
```
